128 devices in a mesh: island: 8 (over y, x_hi), fsdp: 16 (over z, x_lo, core).
Axes of the slice: x: 4 (x_hi: 2, x_lo: 2; x = x_hi * 2 + x_lo), y: 4, z: 4, core: 2. Of those that a mesh axis runs over, the one named last changes fastest.
Arguments:
- features: bfloat16 [8, 16384, 4096], P('island', 'fsdp'), may hold values from -6 to 6
- upstream: bfloat16 [8, 16384, 1024], P('island', 'fsdp'), may hold values from -0.046875 to 0.046875
- local_weights: float32 [8, 2, 4096, 512], P('island', None, 'fsdp'), may hold values from -6 to 6
- first_moment: float32 [8, 2, 4096, 512], P('island', None, 'fsdp'), may hold values from -4 to 4
- second_moment: float32 [8, 2, 4096, 512], P('island', None, 'fsdp'), may hold values from 0.1 to 1
- anchor: float32 [2, 4096, 512], P(None, 'fsdp'), may hold values from -6 to 6
- outer_momentum: float32 [2, 4096, 512], P(None, 'fsdp'), may hold values from -4 to 4
- fragment: int32 [1], replicated, may hold values from 0 to 7
Outputs:
- weights_out: float32 [8, 2, 4096, 512], P('island', None, 'fsdp')
- first_out: float32 [8, 2, 4096, 512], P('island', None, 'fsdp')
- second_out: float32 [8, 2, 4096, 512], P('island', None, 'fsdp')
- anchor_out: float32 [2, 4096, 512], P(None, 'fsdp')
- momentum_out: float32 [2, 4096, 512], P(None, 'fsdp')
The draws below stay inside these ranges and needn't reach their ends.
All inputs are finite; a program needn't handle non-finite values.
Results may differ from the reference program's by a relative error of at most 0.0003.
Values may be sent and summed in bfloat16 or wider, within the bound.
A program may use at most 192 MiB of HBM per device.

```python
import math
import jax
import jax.numpy as jnp
from jax import lax

DW = 4096
KW = 512
HEAD = 128
FRAGS = 2
ISL_TOK = 16384
N_ISLAND = 8


def strengthened(result, rng, source, target, shards_of, factor):
    def block_of(position):
        return (jnp.arange(result.shape[position]) // (result.shape[position] // shards_of)).reshape((-1,) + (1,) * (result.ndim - 1 - position))

    first = jax.random.permutation(rng, shards_of)[block_of(target)]
    far = (block_of(target) + shards_of // 2) % shards_of
    return jnp.where((block_of(source) == first) | (block_of(source) == far), factor * result, result)


def steps_of(stream_key, extent, split, least, top_value):
    def one(position, shards_of):
        heights = jax.random.uniform(jax.random.fold_in(jax.random.fold_in(stream_key, 6), position), (shards_of,), jnp.float32, least / len(split), top_value / len(split))
        return jnp.repeat(jnp.exp(heights), extent[position] // shards_of).reshape((-1,) + (1,) * (len(extent) - position - 1))

    gain = one(*split[0])
    for cut in split[1:]:
        gain = gain * one(*cut)
    return gain


def gaussian(key, shape, spread, limit, split=(), held_as=jnp.bfloat16):
    factor_of = steps_of(key, shape, split, -0.22, 0.18) if split else 1.0
    drawn = jax.random.normal(key, shape, jnp.float32) * spread * factor_of
    return jnp.minimum(jnp.maximum(drawn, -limit), limit).astype(held_as)


def gaussian_with(own_key, extent, deviation, reach, shards, heavy, held_as=jnp.bfloat16):
    array = deviation * jax.random.normal(own_key, extent, jnp.float32)
    if shards:
        array = array * steps_of(own_key, extent, shards, -0.22, 0.18)
    return jnp.clip(strengthened(array, jax.random.fold_in(own_key, 3), *heavy), -reach, reach).astype(held_as)


def setup_inputs(seed: int = 0) -> dict:
    seeds = jax.random.split(jax.random.key(seed), 9)
    features = gaussian_with(seeds[0], (N_ISLAND, ISL_TOK, DW), 1.0, 6.0, ((0, 8), (1, 16)), (1, 2, 16, 2.0))
    upstream = gaussian(seeds[1], (N_ISLAND, ISL_TOK, 2 * KW), ISL_TOK ** -0.5, 0.046875, ((0, 8), (1, 16)))
    local_weights = gaussian(seeds[2], (N_ISLAND, FRAGS, DW, KW), 1.0, 6.0, ((0, 8), (2, 16)), jnp.float32)
    first_moment = gaussian(seeds[3], (N_ISLAND, FRAGS, DW, KW), 0.5, 4.0, ((0, 8), (2, 16)), jnp.float32)
    second_moment = jnp.clip(jnp.exp(math.log(1.0) - 2.3025851 * jax.random.uniform(seeds[4], (N_ISLAND, FRAGS, DW, KW), jnp.float32) ** steps_of(seeds[4], (N_ISLAND, FRAGS, DW, KW), ((0, 8), (2, 16)), -0.2, 0.2)), 0.1, 1.0)
    anchor = gaussian(seeds[5], (FRAGS, DW, KW), 1.0, 6.0, ((1, 16),), jnp.float32)
    outer_momentum = gaussian(seeds[6], (FRAGS, DW, KW), 0.5, 4.0, ((1, 16),), jnp.float32)
    fragment = jax.random.randint(seeds[7], (1,), 0, FRAGS * KW // HEAD).astype(jnp.int32)
    return dict(features=features, upstream=upstream, local_weights=local_weights, first_moment=first_moment, second_moment=second_moment, anchor=anchor, outer_momentum=outer_momentum, fragment=fragment)


def island_grad(pair):
    feats, cots = pair
    contract = (((0,), (0,)), ((), ()))
    return lax.dot_general(feats, cots, contract, preferred_element_type=jnp.float32)

def reference(features, upstream, local_weights, first_moment, second_moment, anchor, outer_momentum, fragment):
    heads = KW // HEAD
    index = fragment[0].astype(jnp.int32)
    proj_index = index // heads
    column = (index % heads * HEAD).astype(jnp.int32)
    proj = (jnp.arange(FRAGS) == proj_index)[:, None, None]
    colmask = (jnp.arange(KW) // HEAD == index % heads)[None, None, :]
    chosen = jnp.logical_and(proj, colmask)
    anchor_p = lax.optimization_barrier(jnp.sum(jnp.where(proj, anchor, 0.0), axis=0))
    moment_p = lax.optimization_barrier(jnp.sum(jnp.where(proj, outer_momentum, 0.0), axis=0))
    own_p = lax.optimization_barrier(jnp.sum(jnp.where(proj[None], local_weights, 0.0), axis=1))
    anchor_f = lax.dynamic_slice_in_dim(anchor_p, column, HEAD, 1)
    moment_f = lax.dynamic_slice_in_dim(moment_p, column, HEAD, 1)
    own_f = lax.dynamic_slice_in_dim(own_p, column, HEAD, 2)
    drift = lax.optimization_barrier(jnp.sum(anchor_f[None] - own_f, axis=0)) / N_ISLAND
    new_moment = 0.9 * moment_f + drift
    merged = anchor_f - 0.7 * (0.9 * new_moment + drift)
    merged_p = lax.dynamic_update_slice_in_dim(anchor_p, merged, column, 1)
    moment_new_p = lax.dynamic_update_slice_in_dim(moment_p, new_moment, column, 1)
    momentum_out = jnp.where(chosen, moment_new_p[None], outer_momentum)
    anchor_out = jnp.where(chosen, merged_p[None], anchor)
    start = jnp.where(chosen[None], merged_p[None, None], local_weights)
    grads = lax.map(island_grad, (features, upstream))
    grads = grads.reshape(N_ISLAND, DW, FRAGS, KW).transpose(0, 2, 1, 3)
    first_out = 0.9 * first_moment + 0.1 * grads
    second_out = 0.95 * second_moment + 0.05 * grads * grads
    weights_out = start - 0.02 * (first_out / (jnp.sqrt(second_out) + 1e-08) + 0.1 * start)
    return (weights_out, first_out, second_out, anchor_out, momentum_out)
```

```python
import functools

import jax
import jax.numpy as jnp
from jax import lax
from jax.experimental import pallas as pl
from jax.experimental.pallas import tpu as pltpu
from jax.sharding import PartitionSpec as P

HEAD = 128
LANES = 128
TOP = 32766.0
TINY = 1e-30
F32 = jnp.float32
MESH = pl.DeviceIdType.MESH


def encode(value, codes, scales):
    @pl.loop(0, codes.shape[1] // LANES)
    def _(j):
        lanes = pl.ds(pl.multiple_of(j * LANES, LANES), LANES)
        v = value(lanes)
        top = jnp.maximum(jnp.max(jnp.abs(v), axis=0, keepdims=True), TINY)
        scales[:, lanes] = top * (1.0 / TOP)
        codes[:, lanes] = jnp.round(v * (TOP / top)).astype(jnp.int32).astype(jnp.int16)


def decode(codes, scales, lanes):
    return codes[:, lanes].astype(jnp.int32).astype(F32) * scales[:, lanes]


def grad_kernel(
    rows, zrows, x_hbm, u_hbm, lw_hbm, frag, grad, total,
    xb, ub, lwb, part, own, core_in,
    zq, zs, zq_in, zs_in, wq, ws, wq_in, ws_in,
    xq, xs, xq_in, xs_in, yq, ys, yq_in, ys_in,
    mine, slots, half_sum, half_in,
    load_sem, core_ss, core_rs, z_ss, z_rs, w_ss, w_rs, x_ss, x_rs, y_ss, y_rs, d_ss, d_rs,
):
    isl, place = lax.axis_index("island"), lax.axis_index("fsdp")
    z, x, c = place // 4, place // 2 % 2, place % 2
    y, h = isl // 2, isl % 2
    half = grad.shape[2]
    quarter = rows // 4

    def at(dz=0, dx=0, dc=0):
        return (isl, (z + dz) % 4 * 4 + (x + dx) % 2 * 2 + (c + dc) % 2)

    def island(dy=0, dh=0):
        return ((y + dy) % 4 * 2 + (h + dh) % 2, place)

    def order(k):
        dz = jnp.where(k < 2, 2, jnp.where(k >= 6, 0, jnp.where(k % 2 == 0, 1, 3)))
        dx = jnp.where(k < 2, 1 - k, jnp.where(k < 4, 1, jnp.where(k < 6, 0, 7 - k)))
        return (z + dz) % 4 * 2 + (x + dx) % 2

    def load_x(k):
        chip = pl.ds(pl.multiple_of(order(k) * 2 * rows, 2 * rows), 2 * rows)
        return pltpu.make_async_copy(x_hbm.at[0, :, chip], xb.at[:, chip], load_sem.at[k])

    load_u = pltpu.make_async_copy(u_hbm.at[0], ub, load_sem.at[8])
    load_lw = pltpu.make_async_copy(lw_hbm.at[0], lwb, load_sem.at[9])
    load_u.start()

    @pl.loop(0, 8)
    def _(k):
        load_x(k).start()

    load_lw.start()

    barrier = pltpu.get_barrier_semaphore()
    peers = [at(dc=1), at(dx=1), at(dz=1), at(dz=3), island(1), island(2), island(3), island(dh=1)]
    for peer in peers:
        pl.semaphore_signal(barrier, inc=1, device_id=peer, device_id_type=MESH)

    def remote(src, dst, ss, rs, peer):
        return pltpu.make_async_remote_copy(
            src_ref=src, dst_ref=dst, send_sem=ss, recv_sem=rs, device_id=peer, device_id_type=MESH
        )

    def term(k, core):
        offset = pl.multiple_of((order(k) * 2 + core) * rows, rows)
        return lax.dot_general(
            xb[:, pl.ds(offset, rows)], ub[...], (((0,), (0,)), ((), ())), preferred_element_type=F32
        )

    def core_copy(k):
        return remote(part.at[k], core_in.at[k], core_ss.at[k], core_rs.at[k], at(dc=1))

    def z_copy(d, s):
        peer = at(dz=1 if d == 0 else 3)
        return (
            remote(zq.at[d, s], zq_in.at[d, s], z_ss.at[d, s, 0], z_rs.at[d, s, 0], peer),
            remote(zs.at[d, s], zs_in.at[d, s], z_ss.at[d, s, 1], z_rs.at[d, s, 1], peer),
        )

    def w_copy(d, s):
        peer = at(dz=1 if d == 0 else 3)
        return (
            remote(wq.at[d, s], wq_in.at[d, s], w_ss.at[d, s, 0], w_rs.at[d, s, 0], peer),
            remote(ws.at[d, s], ws_in.at[d, s], w_ss.at[d, s, 1], w_rs.at[d, s, 1], peer),
        )

    def x_copy(s):
        peer = at(dx=1)
        return (
            remote(xq.at[s], xq_in.at[s], x_ss.at[s, 0], x_rs.at[s, 0], peer),
            remote(xs.at[s], xs_in.at[s], x_ss.at[s, 1], x_rs.at[s, 1], peer),
        )

    def y_copy():
        peer = at(dx=1)
        return (
            remote(yq, yq_in, y_ss.at[0], y_rs.at[0], peer),
            remote(ys, ys_in, y_ss.at[1], y_rs.at[1], peer),
        )

    def start(pair):
        for copy in pair:
            copy.start()

    def arrive(pair):
        for copy in pair:
            copy.wait_recv()

    def shifted(lanes, columns):
        return pl.ds(pl.multiple_of(lanes.start + columns, LANES), LANES)

    def chip_term(k, r, n, side=0):
        def value(lanes):
            lanes = shifted(lanes, side * half)
            return own[k, pl.ds(r, n), lanes] + core_in[k, pl.ds(r, n), lanes]

        return value

    wrows = rows - zrows

    def z_term(k, side):
        return chip_term(k, 0, zrows, side)

    def w_term(k, slot, side):
        base = chip_term(k, zrows, wrows, side)

        def value(lanes):
            return base(lanes) + decode(xq_in.at[slot], xs_in.at[slot], shifted(lanes, side * half))

        return value

    def send_z(d, s, value):
        encode(value, zq.at[d, s], zs.at[d, s])
        start(z_copy(d, s))

    def send_w(d, s, value):
        encode(value, wq.at[d, s], ws.at[d, s])
        start(w_copy(d, s))

    def send_x(s, k):
        encode(chip_term(k, zrows, wrows), xq.at[s], xs.at[s])
        start(x_copy(s))

    def z_plus(d, k, got):
        arrive(z_copy(d, got))
        return lambda lanes: z_term(k, d)(lanes) + decode(zq_in.at[d, got], zs_in.at[d, got], lanes)

    load_u.wait()

    @pl.loop(0, 2)
    def _(k):
        load_x(k).wait()
        part[k] = term(k, 1 - c)

        @pl.when(k == 0)
        def _():
            pl.semaphore_wait(barrier, len(peers))

        core_copy(k).start()

    load_lw.wait()
    index = frag[0]
    heads = half // HEAD

    @pl.loop(0, rows // 32)
    def _(j):
        few = pl.ds(pl.multiple_of(j * 32, 32), 32)
        chosen = lwb[0, few, pl.ds(0, HEAD)]
        for g in range(1, heads * lwb.shape[0]):
            chosen = jnp.where(index == g, lwb[g // heads, few, pl.ds(g % heads * HEAD, HEAD)], chosen)
        mine[few, :] = chosen

    def y_rows(dy):
        return pl.ds(pl.multiple_of((y + dy) % 4 * quarter, quarter), quarter)

    def scatter_copy(dy):
        return remote(mine.at[y_rows(dy)], slots.at[dy - 1], d_ss.at[dy - 1], d_rs.at[dy - 1], island(dy))

    def cross_copy():
        return remote(half_sum, half_in, d_ss.at[3], d_rs.at[3], island(dh=1))

    def gather_copy(dy):
        return remote(total.at[y_rows(0)], total.at[y_rows(0)], d_ss.at[3 + dy], d_rs.at[3 + dy], island(dy))

    def gather_arrive(dy):
        rows_in = total.at[y_rows(-dy)]
        return remote(rows_in, rows_in, d_ss.at[3 + dy], d_rs.at[3 + dy], island(dy))

    for dy in (1, 2, 3):
        scatter_copy(dy).start()

    @pl.loop(0, 8)
    def _(k):
        own[k] = term(k, c)

        @pl.when(k < 6)
        def _():
            load_x(k + 2).wait()
            part[k + 2] = term(k + 2, 1 - c)
            core_copy(k + 2).start()

        core_copy(k).wait_recv()

        @pl.when(k == 0)
        def _():
            send_z(0, 0, z_term(0, 0))
            send_z(1, 0, z_term(0, 1))
            send_x(0, 0)

        @pl.when(k == 1)
        def _():
            send_z(0, 1, z_term(1, 0))
            send_z(1, 1, z_term(1, 1))

        @pl.when(k == 2)
        def _():
            send_x(1, 2)
            send_z(0, 2, z_term(2, 1))
            for dy in (1, 2, 3):
                scatter_copy(dy).wait_recv()
            half_sum[...] = mine[y_rows(0), :] + slots[0] + slots[1] + slots[2]
            cross_copy().start()

        @pl.when(k == 3)
        def _():
            send_x(2, 3)
            send_z(1, 2, z_term(3, 0))

        @pl.when(k == 4)
        def _():
            send_z(0, 3, z_plus(0, 2, 0))
            send_z(1, 3, z_plus(1, 3, 0))
            send_z(0, 4, z_term(4, 1))
            cross_copy().wait_recv()
            total[y_rows(0), :] = half_sum[...] + half_in[...]
            for dy in (1, 2, 3):
                gather_copy(dy).start()

        @pl.when(k == 5)
        def _():
            send_z(1, 4, z_term(5, 0))

        @pl.when(k == 6)
        def _():
            send_x(3, 6)

    send_z(0, 5, z_plus(0, 4, 1))
    send_z(1, 5, z_plus(1, 5, 1))

    arrive(x_copy(0))
    send_w(0, 0, w_term(1, 0, 0))
    send_w(1, 0, w_term(1, 0, 1))

    def z_sum(k, leaf, chain, side):
        def value(lanes):
            return (
                z_term(k, side)(lanes)
                + decode(zq_in.at[side, chain], zs_in.at[side, chain], lanes)
                + decode(zq_in.at[1 - side, leaf], zs_in.at[1 - side, leaf], lanes)
            )

        return value

    for d in (0, 1):
        arrive(z_copy(d, 2))
        arrive(z_copy(d, 3))
    for side in (0, 1):
        columns = pl.ds(side * half, half)
        encode(z_sum(6, 2, 3, side), yq.at[:, columns], ys.at[:, columns])
    start(y_copy())

    arrive(x_copy(1))
    send_w(0, 1, w_term(4, 1, 1))
    arrive(x_copy(2))
    send_w(1, 1, w_term(5, 2, 0))
    for d, k, slot in ((0, 4, 1), (1, 5, 2)):
        arrive(w_copy(d, 0))
        base = w_term(k, slot, d)
        send_w(d, 2, lambda lanes, d=d, base=base: base(lanes) + decode(wq_in.at[d, 0], ws_in.at[d, 0], lanes))

    for d in (0, 1):
        arrive(z_copy(d, 4))
        arrive(z_copy(d, 5))
    arrive(x_copy(3))
    arrive(y_copy())
    for side in (0, 1):
        base = z_sum(7, 4, 5, side)

        @pl.loop(0, half // LANES)
        def _(j):
            lanes = pl.ds(pl.multiple_of(j * LANES, LANES), LANES)
            grad[side, pl.ds(0, zrows), lanes] = base(lanes) + decode(yq_in, ys_in, shifted(lanes, side * half))

    for d in (0, 1):
        arrive(w_copy(d, 1))
        arrive(w_copy(d, 2))
    for side in (0, 1):
        base = w_term(7, 3, side)

        @pl.loop(0, half // LANES)
        def _(j):
            lanes = pl.ds(pl.multiple_of(j * LANES, LANES), LANES)
            grad[side, pl.ds(zrows, wrows), lanes] = (
                base(lanes)
                + decode(wq_in.at[side, 2], ws_in.at[side, 2], lanes)
                + decode(wq_in.at[1 - side, 1], ws_in.at[1 - side, 1], lanes)
            )

    for dy in (1, 2, 3):
        gather_arrive(dy).wait_recv()
        gather_copy(dy).wait_send()
        scatter_copy(dy).wait_send()
    cross_copy().wait_send()

    @pl.loop(0, 8)
    def _(k):
        core_copy(k).wait_send()

    pairs = [z_copy(d, s) for d in (0, 1) for s in range(6)] + [w_copy(d, s) for d in (0, 1) for s in range(3)]
    pairs += [x_copy(s) for s in range(4)] + [y_copy()]
    for pair in pairs:
        for copy in pair:
            copy.wait_send()


def update_kernel(
    islands, frag, grad, total, lw, first, second, anchor, moment, lw_out, first_out, second_out, anchor_out, moment_out
):
    index = frag[0]
    heads = lw.shape[3] // HEAD
    proj, column = index // heads, pl.multiple_of(index % heads * HEAD, HEAD)
    anchor_f = anchor[proj, :, pl.ds(column, HEAD)]
    moment_f = moment[proj, :, pl.ds(column, HEAD)]
    drift = anchor_f - total[...] * (1.0 / islands)
    moment_new = 0.9 * moment_f + drift
    merged = anchor_f - 0.7 * (0.9 * moment_new + drift)
    for p in range(lw.shape[1]):
        for j in range(heads):
            here = index == p * heads + j
            lanes = pl.ds(j * HEAD, HEAD)
            anchor_out[p, :, lanes] = jnp.where(here, merged, anchor[p, :, lanes])
            moment_out[p, :, lanes] = jnp.where(here, moment_new, moment[p, :, lanes])
            begin = jnp.where(here, merged, lw[0, p, :, lanes])
            g = grad[p, :, lanes]
            m = 0.9 * first[0, p, :, lanes] + 0.1 * g
            v = 0.95 * second[0, p, :, lanes] + 0.05 * g * g
            first_out[0, p, :, lanes] = m
            second_out[0, p, :, lanes] = v
            lw_out[0, p, :, lanes] = begin - 0.02 * (m / (jnp.sqrt(v) + 1e-08) + 0.1 * begin)


def body(features, upstream, local_weights, first_moment, second_moment, anchor, outer_momentum, fragment):
    _, tokens, width = features.shape
    _, frags, rows, half = local_weights.shape
    cols = frags * half
    zrows = rows * 9 // 16
    wrows = rows - zrows
    i16 = jnp.int16

    def vm(shape, dtype):
        return pltpu.VMEM(shape, dtype)

    def both(*shape):
        return [vm(shape, i16), vm(shape[:-2] + (1, shape[-1]), F32)] * 2

    def sems(*shape):
        return pltpu.SemaphoreType.DMA(shape)

    any_space = pl.BlockSpec(memory_space=pl.ANY)
    grad, total = pl.pallas_call(
        functools.partial(grad_kernel, rows, zrows),
        out_shape=(
            jax.ShapeDtypeStruct((frags, rows, half), F32),
            jax.ShapeDtypeStruct((rows, HEAD), F32),
        ),
        in_specs=[any_space, any_space, any_space, pl.BlockSpec(memory_space=pltpu.SMEM)],
        out_specs=(pl.BlockSpec(memory_space=pltpu.VMEM), pl.BlockSpec(memory_space=pltpu.VMEM)),
        scratch_shapes=[
            vm((tokens, width), jnp.bfloat16),
            vm((tokens, cols), jnp.bfloat16),
            vm((frags, rows, half), F32),
            vm((8, rows, cols), F32),
            vm((8, rows, cols), F32),
            vm((8, rows, cols), F32),
            *both(2, 6, zrows, half),
            *both(2, 3, wrows, half),
            *both(4, wrows, cols),
            *both(zrows, cols),
            vm((rows, HEAD), F32),
            vm((3, rows // 4, HEAD), F32),
            vm((rows // 4, HEAD), F32),
            vm((rows // 4, HEAD), F32),
            sems(10),
            sems(8),
            sems(8),
            sems(2, 6, 2),
            sems(2, 6, 2),
            sems(2, 3, 2),
            sems(2, 3, 2),
            sems(4, 2),
            sems(4, 2),
            sems(2),
            sems(2),
            sems(7),
            sems(7),
        ],
        compiler_params=pltpu.CompilerParams(
            collective_id=0, has_side_effects=True, vmem_limit_bytes=56 * 2**20
        ),
    )(features, upstream, local_weights, fragment)

    step = rows // 4
    state = pl.BlockSpec((1, frags, step, half), lambda i: (0, 0, i, 0))
    shared = pl.BlockSpec((frags, step, half), lambda i: (0, i, 0))
    weights_shape = jax.ShapeDtypeStruct(local_weights.shape, F32)
    anchor_shape = jax.ShapeDtypeStruct(anchor.shape, F32)
    return pl.pallas_call(
        functools.partial(update_kernel, lax.axis_size("island")),
        grid=(4,),
        out_shape=(weights_shape, weights_shape, weights_shape, anchor_shape, anchor_shape),
        in_specs=[
            pl.BlockSpec(memory_space=pltpu.SMEM),
            shared,
            pl.BlockSpec((step, HEAD), lambda i: (i, 0)),
            state,
            state,
            state,
            shared,
            shared,
        ],
        out_specs=(state, state, state, shared, shared),
        compiler_params=pltpu.CompilerParams(vmem_limit_bytes=16 * 2**20),
    )(fragment, grad, total, local_weights, first_moment, second_moment, anchor, outer_momentum)


def solution(mesh):
    placed = (
        P("island", "fsdp", None),
        P("island", "fsdp", None),
        P("island", None, "fsdp", None),
        P("island", None, "fsdp", None),
        P("island", None, "fsdp", None),
        P(None, "fsdp", None),
        P(None, "fsdp", None),
        P(),
    )
    return jax.shard_map(
        body,
        mesh=mesh,
        in_specs=placed,
        out_specs=(
            P("island", None, "fsdp", None),
            P("island", None, "fsdp", None),
            P("island", None, "fsdp", None),
            P(None, "fsdp", None),
            P(None, "fsdp", None),
        ),
        check_vma=False,
    )
```

```python
import functools

import jax
import jax.numpy as jnp
from jax import lax
from jax.experimental import pallas as pl
from jax.experimental.pallas import tpu as pltpu
from jax.sharding import PartitionSpec as P

HEAD = 128
LANES = 128
TOP = 32766.0
TINY = 1e-30
F32 = jnp.float32
MESH = pl.DeviceIdType.MESH


def encode(value, codes, scales):
    @pl.loop(0, codes.shape[1] // LANES)
    def _(j):
        lanes = pl.ds(pl.multiple_of(j * LANES, LANES), LANES)
        v = value(lanes)
        top = jnp.maximum(jnp.max(jnp.abs(v), axis=0, keepdims=True), TINY)
        scales[:, lanes] = top * (1.0 / TOP)
        codes[:, lanes] = jnp.round(v * (TOP / top)).astype(jnp.int32).astype(jnp.int16)


def decode(codes, scales, lanes):
    return codes[:, lanes].astype(jnp.int32).astype(F32) * scales[:, lanes]


def grad_kernel(
    rows, zrows, x_hbm, u_hbm, lw_hbm, first_hbm, second_hbm, anchor_hbm, moment_hbm, frag,
    grad, total, lwb, firstb, secondb, anchorb, momentb,
    xb, ub, part, own, core_in,
    zq, zs, zq_in, zs_in, wq, ws, wq_in, ws_in,
    xq, xs, xq_in, xs_in, yq, ys, yq_in, ys_in,
    mine, slots, half_sum, half_in,
    load_sem, core_ss, core_rs, z_ss, z_rs, w_ss, w_rs, x_ss, x_rs, y_ss, y_rs, d_ss, d_rs,
):
    isl, place = lax.axis_index("island"), lax.axis_index("fsdp")
    z, x, c = place // 4, place // 2 % 2, place % 2
    y, h = isl // 2, isl % 2
    half = grad.shape[2]
    quarter = rows // 4

    def at(dz=0, dx=0, dc=0):
        return (isl, (z + dz) % 4 * 4 + (x + dx) % 2 * 2 + (c + dc) % 2)

    def island(dy=0, dh=0):
        return ((y + dy) % 4 * 2 + (h + dh) % 2, place)

    def order(k):
        dz = jnp.where(k < 2, 2, jnp.where(k >= 6, 0, jnp.where(k % 2 == 0, 1, 3)))
        dx = jnp.where(k < 2, 1 - k, jnp.where(k < 4, 1, jnp.where(k < 6, 0, 7 - k)))
        return (z + dz) % 4 * 2 + (x + dx) % 2

    def load_x(k):
        chip = pl.ds(pl.multiple_of(order(k) * 2 * rows, 2 * rows), 2 * rows)
        return pltpu.make_async_copy(x_hbm.at[0, :, chip], xb.at[:, chip], load_sem.at[k])

    load_u = pltpu.make_async_copy(u_hbm.at[0], ub, load_sem.at[8])
    load_lw = pltpu.make_async_copy(lw_hbm, lwb, load_sem.at[9])
    rest = ((first_hbm, firstb), (second_hbm, secondb), (anchor_hbm, anchorb), (moment_hbm, momentb))
    load_rest = [pltpu.make_async_copy(src, dst, load_sem.at[10 + n]) for n, (src, dst) in enumerate(rest)]
    load_u.start()

    @pl.loop(0, 8)
    def _(k):
        load_x(k).start()

    load_lw.start()

    barrier = pltpu.get_barrier_semaphore()
    peers = [at(dc=1), at(dx=1), at(dz=1), at(dz=3), island(1), island(2), island(3), island(dh=1)]
    for peer in peers:
        pl.semaphore_signal(barrier, inc=1, device_id=peer, device_id_type=MESH)

    def remote(src, dst, ss, rs, peer):
        return pltpu.make_async_remote_copy(
            src_ref=src, dst_ref=dst, send_sem=ss, recv_sem=rs, device_id=peer, device_id_type=MESH
        )

    def term(k, core):
        offset = pl.multiple_of((order(k) * 2 + core) * rows, rows)
        return lax.dot_general(
            xb[:, pl.ds(offset, rows)], ub[...], (((0,), (0,)), ((), ())), preferred_element_type=F32
        )

    def core_copy(k):
        return remote(part.at[k], core_in.at[k], core_ss.at[k], core_rs.at[k], at(dc=1))

    def z_copy(d, s):
        peer = at(dz=1 if d == 0 else 3)
        return (
            remote(zq.at[d, s], zq_in.at[d, s], z_ss.at[d, s, 0], z_rs.at[d, s, 0], peer),
            remote(zs.at[d, s], zs_in.at[d, s], z_ss.at[d, s, 1], z_rs.at[d, s, 1], peer),
        )

    def w_copy(d, s):
        peer = at(dz=1 if d == 0 else 3)
        return (
            remote(wq.at[d, s], wq_in.at[d, s], w_ss.at[d, s, 0], w_rs.at[d, s, 0], peer),
            remote(ws.at[d, s], ws_in.at[d, s], w_ss.at[d, s, 1], w_rs.at[d, s, 1], peer),
        )

    def x_copy(s):
        peer = at(dx=1)
        return (
            remote(xq.at[s], xq_in.at[s], x_ss.at[s, 0], x_rs.at[s, 0], peer),
            remote(xs.at[s], xs_in.at[s], x_ss.at[s, 1], x_rs.at[s, 1], peer),
        )

    def y_copy():
        peer = at(dx=1)
        return (
            remote(yq, yq_in, y_ss.at[0], y_rs.at[0], peer),
            remote(ys, ys_in, y_ss.at[1], y_rs.at[1], peer),
        )

    def start(pair):
        for copy in pair:
            copy.start()

    def arrive(pair):
        for copy in pair:
            copy.wait_recv()

    def shifted(lanes, columns):
        return pl.ds(pl.multiple_of(lanes.start + columns, LANES), LANES)

    def chip_term(k, r, n, side=0):
        def value(lanes):
            lanes = shifted(lanes, side * half)
            return own[k, pl.ds(r, n), lanes] + core_in[k, pl.ds(r, n), lanes]

        return value

    wrows = rows - zrows

    def z_term(k, side):
        return chip_term(k, 0, zrows, side)

    def w_term(k, slot, side):
        base = chip_term(k, zrows, wrows, side)

        def value(lanes):
            return base(lanes) + decode(xq_in.at[slot], xs_in.at[slot], shifted(lanes, side * half))

        return value

    def send_z(d, s, value):
        encode(value, zq.at[d, s], zs.at[d, s])
        start(z_copy(d, s))

    def send_w(d, s, value):
        encode(value, wq.at[d, s], ws.at[d, s])
        start(w_copy(d, s))

    def send_x(s, k):
        encode(chip_term(k, zrows, wrows), xq.at[s], xs.at[s])
        start(x_copy(s))

    def z_plus(d, k, got):
        arrive(z_copy(d, got))
        return lambda lanes: z_term(k, d)(lanes) + decode(zq_in.at[d, got], zs_in.at[d, got], lanes)

    load_u.wait()

    @pl.loop(0, 2)
    def _(k):
        load_x(k).wait()
        part[k] = term(k, 1 - c)

        @pl.when(k == 0)
        def _():
            pl.semaphore_wait(barrier, len(peers))

        core_copy(k).start()

    load_lw.wait()
    index = frag[0]
    heads = half // HEAD

    @pl.loop(0, rows // 32)
    def _(j):
        few = pl.ds(pl.multiple_of(j * 32, 32), 32)
        chosen = lwb[0, 0, few, pl.ds(0, HEAD)]
        for g in range(1, heads * lwb.shape[1]):
            chosen = jnp.where(index == g, lwb[0, g // heads, few, pl.ds(g % heads * HEAD, HEAD)], chosen)
        mine[few, :] = chosen

    def y_rows(dy):
        return pl.ds(pl.multiple_of((y + dy) % 4 * quarter, quarter), quarter)

    def scatter_copy(dy):
        return remote(mine.at[y_rows(dy)], slots.at[dy - 1], d_ss.at[dy - 1], d_rs.at[dy - 1], island(dy))

    def cross_copy():
        return remote(half_sum, half_in, d_ss.at[3], d_rs.at[3], island(dh=1))

    def gather_copy(dy):
        return remote(total.at[y_rows(0)], total.at[y_rows(0)], d_ss.at[3 + dy], d_rs.at[3 + dy], island(dy))

    def gather_arrive(dy):
        rows_in = total.at[y_rows(-dy)]
        return remote(rows_in, rows_in, d_ss.at[3 + dy], d_rs.at[3 + dy], island(dy))

    for dy in (1, 2, 3):
        scatter_copy(dy).start()
    for copy in load_rest:
        copy.start()

    def z_sum(k, leaf, chain, side):
        def value(lanes):
            return (
                z_term(k, side)(lanes)
                + decode(zq_in.at[side, chain], zs_in.at[side, chain], lanes)
                + decode(zq_in.at[1 - side, leaf], zs_in.at[1 - side, leaf], lanes)
            )

        return value

    def collect(side, r, n, value):
        @pl.loop(0, half // LANES)
        def _(j):
            lanes = pl.ds(pl.multiple_of(j * LANES, LANES), LANES)
            grad[side, pl.ds(r, n), lanes] = value(lanes)

    def add(side, r, n, value):
        @pl.loop(0, half // LANES)
        def _(j):
            lanes = pl.ds(pl.multiple_of(j * LANES, LANES), LANES)
            grad[side, pl.ds(r, n), lanes] += value(lanes)

    @pl.loop(0, 8)
    def _(k):
        own[k] = term(k, c)

        @pl.when(k < 6)
        def _():
            load_x(k + 2).wait()
            part[k + 2] = term(k + 2, 1 - c)
            core_copy(k + 2).start()

        core_copy(k).wait_recv()

        @pl.when(k == 0)
        def _():
            send_z(0, 0, z_term(0, 0))
            send_z(1, 0, z_term(0, 1))
            send_x(0, 0)

        @pl.when(k == 1)
        def _():
            send_z(0, 1, z_term(1, 0))
            send_z(1, 1, z_term(1, 1))

        @pl.when(k == 2)
        def _():
            send_x(1, 2)
            send_z(0, 2, z_term(2, 1))
            for dy in (1, 2, 3):
                scatter_copy(dy).wait_recv()
            half_sum[...] = mine[y_rows(0), :] + slots[0] + slots[1] + slots[2]
            cross_copy().start()

        @pl.when(k == 3)
        def _():
            send_z(1, 2, z_term(3, 0))
            send_x(2, 3)
            send_z(0, 3, z_plus(0, 2, 0))
            send_z(1, 3, z_plus(1, 3, 0))

        @pl.when(k == 4)
        def _():
            send_z(0, 4, z_term(4, 1))
            cross_copy().wait_recv()
            total[y_rows(0), :] = half_sum[...] + half_in[...]
            for dy in (1, 2, 3):
                gather_copy(dy).start()

        @pl.when(k == 5)
        def _():
            send_z(1, 4, z_term(5, 0))
            arrive(x_copy(0))
            send_w(0, 0, w_term(1, 0, 0))
            send_w(1, 0, w_term(1, 0, 1))
            send_z(0, 5, z_plus(0, 4, 1))
            send_z(1, 5, z_plus(1, 5, 1))

        @pl.when(k == 6)
        def _():
            send_x(3, 6)
            arrive(x_copy(1))
            send_w(0, 1, w_term(4, 1, 1))

    for d in (0, 1):
        arrive(z_copy(d, 2))
        arrive(z_copy(d, 3))
    for side in (0, 1):
        columns = pl.ds(side * half, half)
        encode(z_sum(6, 2, 3, side), yq.at[:, columns], ys.at[:, columns])
    start(y_copy())

    arrive(x_copy(2))
    send_w(1, 1, w_term(5, 2, 0))
    for d, k, slot in ((0, 4, 1), (1, 5, 2)):
        arrive(w_copy(d, 0))
        base = w_term(k, slot, d)
        send_w(d, 2, lambda lanes, d=d, base=base: base(lanes) + decode(wq_in.at[d, 0], ws_in.at[d, 0], lanes))

    for d in (0, 1):
        arrive(z_copy(d, 4))
        arrive(z_copy(d, 5))
    for side in (0, 1):
        collect(side, 0, zrows, z_sum(7, 4, 5, side))
    arrive(x_copy(3))
    for d in (0, 1):
        arrive(w_copy(d, 1))
    for side in (0, 1):
        base = w_term(7, 3, side)
        collect(
            side, zrows, wrows,
            lambda lanes, side=side, base=base: base(lanes)
            + decode(wq_in.at[1 - side, 1], ws_in.at[1 - side, 1], lanes),
        )
    for d in (0, 1):
        arrive(w_copy(d, 2))
    for side in (0, 1):
        add(side, zrows, wrows, lambda lanes, side=side: decode(wq_in.at[side, 2], ws_in.at[side, 2], lanes))
    arrive(y_copy())
    for side in (0, 1):
        add(side, 0, zrows, lambda lanes, side=side: decode(yq_in, ys_in, shifted(lanes, side * half)))

    for copy in load_rest:
        copy.wait()

    for dy in (1, 2, 3):
        gather_arrive(dy).wait_recv()
        gather_copy(dy).wait_send()
        scatter_copy(dy).wait_send()
    cross_copy().wait_send()

    @pl.loop(0, 8)
    def _(k):
        core_copy(k).wait_send()

    pairs = [z_copy(d, s) for d in (0, 1) for s in range(6)] + [w_copy(d, s) for d in (0, 1) for s in range(3)]
    pairs += [x_copy(s) for s in range(4)] + [y_copy()]
    for pair in pairs:
        for copy in pair:
            copy.wait_send()


def update_kernel(
    islands, step, frag, grad, total, lw, first, second, anchor, moment,
    lw_out, first_out, second_out, anchor_out, moment_out, lw_new, first_new, second_new, anchor_new, moment_new, sems,
):
    index = frag[0]
    rows = lw.shape[2]
    heads = lw.shape[3] // HEAD
    groups = [(p, pl.ds(j * HEAD, HEAD)) for p in range(lw.shape[1]) for j in range(heads)]

    def copies(i):
        some = pl.ds(pl.multiple_of(i * step, step), step)
        pairs = [(lw_new, lw_out.at[0]), (first_new, first_out.at[0]), (second_new, second_out.at[0])]
        pairs += [(anchor_new, anchor_out), (moment_new, moment_out)]
        return [
            pltpu.make_async_copy(src.at[:, some], dst.at[:, some], sems.at[i, n]) for n, (src, dst) in enumerate(pairs)
        ]

    @pl.loop(0, rows // step)
    def _(i):
        some = pl.ds(pl.multiple_of(i * step, step), step)
        anchor_f, moment_f = anchor[0, some, groups[0][1]], moment[0, some, groups[0][1]]
        for g, (p, lanes) in enumerate(groups[1:], 1):
            anchor_f = jnp.where(index == g, anchor[p, some, lanes], anchor_f)
            moment_f = jnp.where(index == g, moment[p, some, lanes], moment_f)
        drift = anchor_f - total[some, :] * (1.0 / islands)
        moment_f = 0.9 * moment_f + drift
        merged = anchor_f - 0.7 * (0.9 * moment_f + drift)
        for g, (p, lanes) in enumerate(groups):
            here = index == g
            anchor_new[p, some, lanes] = jnp.where(here, merged, anchor[p, some, lanes])
            moment_new[p, some, lanes] = jnp.where(here, moment_f, moment[p, some, lanes])
            begin = jnp.where(here, merged, lw[0, p, some, lanes])
            gr = grad[p, some, lanes]
            m = 0.9 * first[0, p, some, lanes] + 0.1 * gr
            v = 0.95 * second[0, p, some, lanes] + 0.05 * gr * gr
            first_new[p, some, lanes] = m
            second_new[p, some, lanes] = v
            lw_new[p, some, lanes] = begin - 0.02 * (m / (jnp.sqrt(v) + 1e-08) + 0.1 * begin)
        for copy in copies(i):
            copy.start()

    @pl.loop(0, rows // step)
    def _(i):
        for copy in copies(i):
            copy.wait()


def body(features, upstream, local_weights, first_moment, second_moment, anchor, outer_momentum, fragment):
    _, tokens, width = features.shape
    _, frags, rows, half = local_weights.shape
    cols = frags * half
    zrows = rows * 9 // 16
    wrows = rows - zrows
    i16 = jnp.int16

    def vm(shape, dtype):
        return pltpu.VMEM(shape, dtype)

    def both(*shape):
        return [vm(shape, i16), vm(shape[:-2] + (1, shape[-1]), F32)] * 2

    def sems(*shape):
        return pltpu.SemaphoreType.DMA(shape)

    states = (local_weights, first_moment, second_moment, anchor, outer_momentum)
    any_space = pl.BlockSpec(memory_space=pl.ANY)
    near = pl.pallas_call(
        functools.partial(grad_kernel, rows, zrows),
        out_shape=(vm((frags, rows, half), F32), vm((rows, HEAD), F32), *[vm(a.shape, F32) for a in states]),
        in_specs=[any_space] * 7 + [pl.BlockSpec(memory_space=pltpu.SMEM)],
        out_specs=[pl.BlockSpec(memory_space=pltpu.VMEM)] * 7,
        scratch_shapes=[
            vm((tokens, width), jnp.bfloat16),
            vm((tokens, cols), jnp.bfloat16),
            vm((8, rows, cols), F32),
            vm((8, rows, cols), F32),
            vm((8, rows, cols), F32),
            *both(2, 6, zrows, half),
            *both(2, 3, wrows, half),
            *both(4, wrows, cols),
            *both(zrows, cols),
            vm((rows, HEAD), F32),
            vm((3, rows // 4, HEAD), F32),
            vm((rows // 4, HEAD), F32),
            vm((rows // 4, HEAD), F32),
            sems(14),
            sems(8),
            sems(8),
            sems(2, 6, 2),
            sems(2, 6, 2),
            sems(2, 3, 2),
            sems(2, 3, 2),
            sems(4, 2),
            sems(4, 2),
            sems(2),
            sems(2),
            sems(7),
            sems(7),
        ],
        compiler_params=pltpu.CompilerParams(
            collective_id=0, has_side_effects=True, vmem_limit_bytes=48 * 2**20
        ),
    )(features, upstream, *states, fragment)

    step = rows // 8
    weights_shape = jax.ShapeDtypeStruct(local_weights.shape, F32)
    anchor_shape = jax.ShapeDtypeStruct(anchor.shape, F32)
    return pl.pallas_call(
        functools.partial(update_kernel, lax.axis_size("island"), step),
        out_shape=(weights_shape, weights_shape, weights_shape, anchor_shape, anchor_shape),
        in_specs=[pl.BlockSpec(memory_space=pltpu.SMEM)] + [pl.BlockSpec(memory_space=pltpu.VMEM)] * 7,
        out_specs=[any_space] * 5,
        scratch_shapes=[vm((frags, rows, half), F32)] * 5 + [sems(8, 5)],
        compiler_params=pltpu.CompilerParams(vmem_limit_bytes=16 * 2**20),
    )(fragment, *[pltpu.with_memory_space_constraint(a, pltpu.VMEM) for a in near])


def solution(mesh):
    placed = (
        P("island", "fsdp", None),
        P("island", "fsdp", None),
        P("island", None, "fsdp", None),
        P("island", None, "fsdp", None),
        P("island", None, "fsdp", None),
        P(None, "fsdp", None),
        P(None, "fsdp", None),
        P(),
    )
    return jax.shard_map(
        body,
        mesh=mesh,
        in_specs=placed,
        out_specs=(
            P("island", None, "fsdp", None),
            P("island", None, "fsdp", None),
            P("island", None, "fsdp", None),
            P(None, "fsdp", None),
            P(None, "fsdp", None),
        ),
        check_vma=False,
    )
```

```python
import functools

import jax
import jax.numpy as jnp
from jax import lax
from jax.experimental import pallas as pl
from jax.experimental.pallas import tpu as pltpu
from jax.sharding import PartitionSpec as P

HEAD = 128
LANES = 128
TOP = 32766.0
TINY = 1e-30
F32 = jnp.float32
MESH = pl.DeviceIdType.MESH


def encode(value, codes, scales):
    @pl.loop(0, codes.shape[1] // LANES)
    def _(j):
        lanes = pl.ds(pl.multiple_of(j * LANES, LANES), LANES)
        v = value(lanes)
        top = jnp.maximum(jnp.max(jnp.abs(v), axis=0, keepdims=True), TINY)
        scales[:, lanes] = top * (1.0 / TOP)
        codes[:, lanes] = jnp.round(v * (TOP / top)).astype(jnp.int32).astype(jnp.int16)


def decode(codes, scales, lanes):
    return codes[:, lanes].astype(jnp.int32).astype(F32) * scales[:, lanes]


def grad_kernel(
    islands, rows, zrows, x_hbm, u_hbm, lw_hbm, first_hbm, second_hbm, anchor_hbm, moment_hbm, frag,
    grad, lwb, firstb, secondb, anchorb, momentb,
    xb, ub, part, own, core_in,
    zq, zs, zq_in, zs_in, wq, ws, wq_in, ws_in,
    xq, xs, xq_in, xs_in, yq, ys, yq_in, ys_in,
    mine, slots, half_sum, half_in, total,
    load_sem, state_sem, core_ss, core_rs, z_ss, z_rs, w_ss, w_rs, x_ss, x_rs, y_ss, y_rs, d_ss, d_rs,
):
    isl, place = lax.axis_index("island"), lax.axis_index("fsdp")
    z, x, c = place // 4, place // 2 % 2, place % 2
    y, h = isl // 2, isl % 2
    half = grad.shape[2]
    quarter = rows // 4

    def at(dz=0, dx=0, dc=0):
        return (isl, (z + dz) % 4 * 4 + (x + dx) % 2 * 2 + (c + dc) % 2)

    def island(dy=0, dh=0):
        return ((y + dy) % 4 * 2 + (h + dh) % 2, place)

    def order(k):
        dz = jnp.where(k < 2, 2, jnp.where(k >= 6, 0, jnp.where(k % 2 == 0, 1, 3)))
        dx = jnp.where(k < 2, 1 - k, jnp.where(k < 4, 1, jnp.where(k < 6, 0, 7 - k)))
        return (z + dz) % 4 * 2 + (x + dx) % 2

    def block(k, core):
        return pl.ds(pl.multiple_of((order(k) * 2 + core) * rows, rows), rows)

    def load_x(k, core):
        columns = block(k, (c + core) % 2)
        return pltpu.make_async_copy(x_hbm.at[0, :, columns], xb.at[:, columns], load_sem.at[k, core])

    def load_u(side):
        columns = pl.ds(side * half, half)
        return pltpu.make_async_copy(u_hbm.at[0, :, columns], ub.at[:, columns], load_sem.at[8, side])

    states = ((lw_hbm, lwb), (first_hbm, firstb), (second_hbm, secondb), (anchor_hbm, anchorb), (moment_hbm, momentb))
    load_states = [pltpu.make_async_copy(src, dst, state_sem.at[n]) for n, (src, dst) in enumerate(states)]
    load_u(0).start()
    load_x(0, 1).start()
    load_u(1).start()
    load_x(0, 0).start()

    barrier = pltpu.get_barrier_semaphore()
    peers = [at(dc=1), at(dx=1), at(dz=1), at(dz=3), island(1), island(2), island(3), island(dh=1)]
    for peer in peers:
        pl.semaphore_signal(barrier, inc=1, device_id=peer, device_id_type=MESH)

    def remote(src, dst, ss, rs, peer):
        return pltpu.make_async_remote_copy(
            src_ref=src, dst_ref=dst, send_sem=ss, recv_sem=rs, device_id=peer, device_id_type=MESH
        )

    def term(k, core, side=None):
        columns = pl.ds(0, 2 * half) if side is None else pl.ds(side * half, half)
        return lax.dot_general(
            xb[:, block(k, core)], ub[:, columns], (((0,), (0,)), ((), ())), preferred_element_type=F32
        )

    def store(terms, k, value):
        for side in (0, 1):
            terms[k, side] = value[:, side * half : (side + 1) * half]

    def core_copy(k, side):
        return remote(part.at[k, side], core_in.at[k, side], core_ss.at[k, side], core_rs.at[k, side], at(dc=1))

    def z_copy(d, s):
        peer = at(dz=1 if d == 0 else 3)
        return (
            remote(zq.at[d, s], zq_in.at[d, s], z_ss.at[d, s, 0], z_rs.at[d, s, 0], peer),
            remote(zs.at[d, s], zs_in.at[d, s], z_ss.at[d, s, 1], z_rs.at[d, s, 1], peer),
        )

    def w_copy(d, s):
        peer = at(dz=1 if d == 0 else 3)
        return (
            remote(wq.at[d, s], wq_in.at[d, s], w_ss.at[d, s, 0], w_rs.at[d, s, 0], peer),
            remote(ws.at[d, s], ws_in.at[d, s], w_ss.at[d, s, 1], w_rs.at[d, s, 1], peer),
        )

    def x_copy(s, side):
        peer = at(dx=1)
        return (
            remote(xq.at[s, side], xq_in.at[s, side], x_ss.at[s, side, 0], x_rs.at[s, side, 0], peer),
            remote(xs.at[s, side], xs_in.at[s, side], x_ss.at[s, side, 1], x_rs.at[s, side, 1], peer),
        )

    def y_copy(side):
        peer = at(dx=1)
        return (
            remote(yq.at[side], yq_in.at[side], y_ss.at[side, 0], y_rs.at[side, 0], peer),
            remote(ys.at[side], ys_in.at[side], y_ss.at[side, 1], y_rs.at[side, 1], peer),
        )

    def start(pair):
        for copy in pair:
            copy.start()

    def arrive(pair):
        for copy in pair:
            copy.wait_recv()

    def chip_term(k, r, n, side):
        return lambda lanes: own[k, side, pl.ds(r, n), lanes] + core_in[k, side, pl.ds(r, n), lanes]

    wrows = rows - zrows

    def z_term(k, side):
        return chip_term(k, 0, zrows, side)

    def w_term(k, slot, side):
        base = chip_term(k, zrows, wrows, side)

        return lambda lanes: base(lanes) + decode(xq_in.at[slot, side], xs_in.at[slot, side], lanes)

    def send_z(d, s, value):
        encode(value, zq.at[d, s], zs.at[d, s])
        start(z_copy(d, s))

    def send_w(d, s, value):
        encode(value, wq.at[d, s], ws.at[d, s])
        start(w_copy(d, s))

    def send_x(s, k, side):
        encode(chip_term(k, zrows, wrows, side), xq.at[s, side], xs.at[s, side])
        start(x_copy(s, side))

    def z_plus(d, k, got):
        arrive(z_copy(d, got))
        return lambda lanes: z_term(k, d)(lanes) + decode(zq_in.at[d, got], zs_in.at[d, got], lanes)

    load_x(0, 1).wait()
    for side in (0, 1):
        load_u(side).wait()
        part[0, side] = term(0, 1 - c, side)
        if side == 0:
            pl.semaphore_wait(barrier, len(peers))
        core_copy(0, side).start()

    for k in (1, 2):
        load_x(k, 1).start()
        load_x(k, 0).start()
    load_states[0].start()
    load_x(0, 0).wait()
    store(own, 0, term(0, c))
    for side in (0, 1):
        core_copy(0, side).wait_recv()
        send_z(side, 0, z_term(0, side))
        send_x(0, 0, side)

    @pl.loop(3, 8)
    def _(k):
        load_x(k, 1).start()
        load_x(k, 0).start()

    load_x(1, 1).wait()
    store(part, 1, term(1, 1 - c))
    for side in (0, 1):
        core_copy(1, side).start()

    load_states[0].wait()
    index = frag[0]
    heads = half // HEAD
    groups = [(p, pl.ds(j * HEAD, HEAD)) for p in range(lwb.shape[1]) for j in range(heads)]

    def fragment(array, few):
        chosen = array[0, few, groups[0][1]]
        for g, (p, lanes) in enumerate(groups[1:], 1):
            chosen = jnp.where(index == g, array[p, few, lanes], chosen)
        return chosen

    def by_rows(body):
        @pl.loop(0, rows // 32)
        def _(j):
            body(pl.ds(pl.multiple_of(j * 32, 32), 32))

    @by_rows
    def _(few):
        mine[few, :] = fragment(lwb.at[0], few)

    def y_rows(dy):
        return pl.ds(pl.multiple_of((y + dy) % 4 * quarter, quarter), quarter)

    def scatter_copy(dy):
        return remote(mine.at[y_rows(dy)], slots.at[dy - 1], d_ss.at[dy - 1], d_rs.at[dy - 1], island(dy))

    def cross_copy():
        return remote(half_sum, half_in, d_ss.at[3], d_rs.at[3], island(dh=1))

    def gather_copy(dy):
        return remote(total.at[y_rows(0)], total.at[y_rows(0)], d_ss.at[3 + dy], d_rs.at[3 + dy], island(dy))

    def gather_arrive(dy):
        rows_in = total.at[y_rows(-dy)]
        return remote(rows_in, rows_in, d_ss.at[3 + dy], d_rs.at[3 + dy], island(dy))

    for dy in (1, 2, 3):
        scatter_copy(dy).start()
    for copy in load_states[1:]:
        copy.start()

    def z_sum(k, leaf, chain, side):
        def value(lanes):
            return (
                z_term(k, side)(lanes)
                + decode(zq_in.at[side, chain], zs_in.at[side, chain], lanes)
                + decode(zq_in.at[1 - side, leaf], zs_in.at[1 - side, leaf], lanes)
            )

        return value

    def collect(side, r, n, value):
        @pl.loop(0, half // LANES)
        def _(j):
            lanes = pl.ds(pl.multiple_of(j * LANES, LANES), LANES)
            grad[side, pl.ds(r, n), lanes] = value(lanes)

    def add(side, r, n, value):
        @pl.loop(0, half // LANES)
        def _(j):
            lanes = pl.ds(pl.multiple_of(j * LANES, LANES), LANES)
            grad[side, pl.ds(r, n), lanes] += value(lanes)

    @pl.loop(1, 8)
    def _(k):
        @pl.when(k < 7)
        def _():
            load_x(k + 1, 1).wait()
            store(part, k + 1, term(k + 1, 1 - c))
            for side in (0, 1):
                core_copy(k + 1, side).start()

        load_x(k, 0).wait()
        store(own, k, term(k, c))
        for side in (0, 1):
            core_copy(k, side).wait_recv()

        @pl.when(k == 1)
        def _():
            send_z(0, 1, z_term(1, 0))
            send_z(1, 1, z_term(1, 1))

        @pl.when(k == 2)
        def _():
            send_z(0, 2, z_term(2, 1))
            send_x(1, 2, 0)
            send_x(1, 2, 1)

        @pl.when(k == 3)
        def _():
            send_z(1, 2, z_term(3, 0))
            for dy in (1, 2, 3):
                scatter_copy(dy).wait_recv()
            half_sum[...] = mine[y_rows(0), :] + slots[0] + slots[1] + slots[2]
            cross_copy().start()
            send_x(2, 3, 0)
            send_x(2, 3, 1)
            send_z(0, 3, z_plus(0, 2, 0))
            send_z(1, 3, z_plus(1, 3, 0))

        @pl.when(k == 4)
        def _():
            send_z(0, 4, z_term(4, 1))

        @pl.when(k == 5)
        def _():
            send_z(1, 4, z_term(5, 0))
            for d in (0, 1):
                arrive(x_copy(0, d))
                send_w(d, 0, w_term(1, 0, d))
            send_z(0, 5, z_plus(0, 4, 1))
            send_z(1, 5, z_plus(1, 5, 1))

        @pl.when(k == 6)
        def _():
            send_x(3, 6, 0)
            send_x(3, 6, 1)
            arrive(x_copy(1, 0))
            arrive(x_copy(1, 1))
            send_w(0, 1, w_term(4, 1, 1))

    for d in (0, 1):
        arrive(z_copy(d, 2))
        arrive(z_copy(d, 3))
    for side in (0, 1):
        encode(z_sum(6, 2, 3, side), yq.at[side], ys.at[side])
        start(y_copy(side))

    cross_copy().wait_recv()
    total[y_rows(0), :] = half_sum[...] + half_in[...]
    for dy in (1, 2, 3):
        gather_copy(dy).start()

    arrive(x_copy(2, 0))
    arrive(x_copy(2, 1))
    send_w(1, 1, w_term(5, 2, 0))
    for d, k, slot in ((0, 4, 1), (1, 5, 2)):
        arrive(w_copy(d, 0))
        base = w_term(k, slot, d)
        send_w(d, 2, lambda lanes, d=d, base=base: base(lanes) + decode(wq_in.at[d, 0], ws_in.at[d, 0], lanes))

    for dy in (1, 2, 3):
        gather_arrive(dy).wait_recv()
    for copy in load_states[1:]:
        copy.wait()

    @by_rows
    def _(few):
        anchor_f = fragment(anchorb, few)
        drift = anchor_f - total[few, :] * (1.0 / islands)
        moment_f = 0.9 * fragment(momentb, few) + drift
        merged = anchor_f - 0.7 * (0.9 * moment_f + drift)
        for g, (p, lanes) in enumerate(groups):
            here = index == g
            anchorb[p, few, lanes] = jnp.where(here, merged, anchorb[p, few, lanes])
            momentb[p, few, lanes] = jnp.where(here, moment_f, momentb[p, few, lanes])
            lwb[0, p, few, lanes] = jnp.where(here, merged, lwb[0, p, few, lanes])

    for d in (0, 1):
        arrive(z_copy(d, 4))
        arrive(z_copy(d, 5))
    for side in (0, 1):
        collect(side, 0, zrows, z_sum(7, 4, 5, side))
    arrive(x_copy(3, 0))
    arrive(x_copy(3, 1))
    for d in (0, 1):
        arrive(w_copy(d, 1))
    for side in (0, 1):
        base = w_term(7, 3, side)
        collect(
            side, zrows, wrows,
            lambda lanes, side=side, base=base: base(lanes)
            + decode(wq_in.at[1 - side, 1], ws_in.at[1 - side, 1], lanes),
        )
    def finish(pairs):
        for pair in pairs:
            for copy in pair:
                copy.wait_send()

    finish([[scatter_copy(dy), gather_copy(dy)] for dy in (1, 2, 3)] + [[cross_copy()]])

    @pl.loop(0, 8)
    def _(k):
        finish([[core_copy(k, side) for side in (0, 1)]])

    finish([z_copy(d, s) for d in (0, 1) for s in range(6)] + [w_copy(d, s) for d in (0, 1) for s in (0, 1)])
    finish([x_copy(s, side) for s in range(4) for side in (0, 1)])

    for d in (0, 1):
        arrive(w_copy(d, 2))
    for side in (0, 1):
        add(side, zrows, wrows, lambda lanes, side=side: decode(wq_in.at[side, 2], ws_in.at[side, 2], lanes))
    for side in (0, 1):
        arrive(y_copy(side))
        add(side, 0, zrows, lambda lanes, side=side: decode(yq_in.at[side], ys_in.at[side], lanes))

    finish([w_copy(d, 2) for d in (0, 1)] + [y_copy(side) for side in (0, 1)])


def update_kernel(
    step, grad, lw, first, second, anchor, moment,
    lw_out, first_out, second_out, anchor_out, moment_out, lw_new, first_new, second_new, sems, shared_sems,
):
    shared = [
        pltpu.make_async_copy(src, dst, shared_sems.at[n])
        for n, (src, dst) in enumerate(((anchor, anchor_out), (moment, moment_out)))
    ]
    for copy in shared:
        copy.start()
    frags, rows, half = grad.shape
    groups = [(p, pl.ds(j * LANES, LANES)) for p in range(frags) for j in range(half // LANES)]

    def copies(i):
        some = pl.ds(pl.multiple_of(i * step, step), step)
        pairs = [(lw_new, lw_out.at[0]), (first_new, first_out.at[0]), (second_new, second_out.at[0])]
        return [
            pltpu.make_async_copy(src.at[:, some], dst.at[:, some], sems.at[i, n]) for n, (src, dst) in enumerate(pairs)
        ]

    @pl.loop(0, rows // step)
    def _(i):
        some = pl.ds(pl.multiple_of(i * step, step), step)
        for p, lanes in groups:
            gr = grad[p, some, lanes]
            begin = lw[0, p, some, lanes]
            m = 0.9 * first[0, p, some, lanes] + 0.1 * gr
            v = 0.95 * second[0, p, some, lanes] + 0.05 * gr * gr
            first_new[p, some, lanes] = m
            second_new[p, some, lanes] = v
            lw_new[p, some, lanes] = begin - 0.02 * (m / (jnp.sqrt(v) + 1e-08) + 0.1 * begin)
        for copy in copies(i):
            copy.start()

    @pl.loop(0, rows // step)
    def _(i):
        for copy in copies(i):
            copy.wait()

    for copy in shared:
        copy.wait()


def body(features, upstream, local_weights, first_moment, second_moment, anchor, outer_momentum, fragment):
    _, tokens, width = features.shape
    _, frags, rows, half = local_weights.shape
    cols = frags * half
    zrows = rows * 9 // 16
    wrows = rows - zrows
    i16 = jnp.int16

    def vm(shape, dtype):
        return pltpu.VMEM(shape, dtype)

    def both(*shape):
        return [vm(shape, i16), vm(shape[:-2] + (1, shape[-1]), F32)] * 2

    def sems(*shape):
        return pltpu.SemaphoreType.DMA(shape)

    states = (local_weights, first_moment, second_moment, anchor, outer_momentum)
    any_space = pl.BlockSpec(memory_space=pl.ANY)
    near = pl.pallas_call(
        functools.partial(grad_kernel, lax.axis_size("island"), rows, zrows),
        out_shape=(vm((frags, rows, half), F32), *[vm(a.shape, F32) for a in states]),
        in_specs=[any_space] * 7 + [pl.BlockSpec(memory_space=pltpu.SMEM)],
        out_specs=[pl.BlockSpec(memory_space=pltpu.VMEM)] * 6,
        scratch_shapes=[
            vm((tokens, width), jnp.bfloat16),
            vm((tokens, cols), jnp.bfloat16),
            vm((8, frags, rows, half), F32),
            vm((8, frags, rows, half), F32),
            vm((8, frags, rows, half), F32),
            *both(2, 6, zrows, half),
            *both(2, 3, wrows, half),
            *both(4, 2, wrows, half),
            *both(2, zrows, half),
            vm((rows, HEAD), F32),
            vm((3, rows // 4, HEAD), F32),
            vm((rows // 4, HEAD), F32),
            vm((rows // 4, HEAD), F32),
            vm((rows, HEAD), F32),
            sems(9, 2),
            sems(5),
            sems(8, 2),
            sems(8, 2),
            sems(2, 6, 2),
            sems(2, 6, 2),
            sems(2, 3, 2),
            sems(2, 3, 2),
            sems(4, 2, 2),
            sems(4, 2, 2),
            sems(2, 2),
            sems(2, 2),
            sems(7),
            sems(7),
        ],
        compiler_params=pltpu.CompilerParams(
            collective_id=0, has_side_effects=True, vmem_limit_bytes=48 * 2**20
        ),
    )(features, upstream, *states, fragment)

    step = rows // 8
    weights_shape = jax.ShapeDtypeStruct(local_weights.shape, F32)
    anchor_shape = jax.ShapeDtypeStruct(anchor.shape, F32)
    return pl.pallas_call(
        functools.partial(update_kernel, step),
        out_shape=(weights_shape, weights_shape, weights_shape, anchor_shape, anchor_shape),
        in_specs=[pl.BlockSpec(memory_space=pltpu.VMEM)] * 6,
        out_specs=[any_space] * 5,
        scratch_shapes=[vm((frags, rows, half), F32)] * 3 + [sems(8, 3), sems(2)],
        compiler_params=pltpu.CompilerParams(vmem_limit_bytes=16 * 2**20),
    )(*[pltpu.with_memory_space_constraint(a, pltpu.VMEM) for a in near])


def solution(mesh):
    placed = (
        P("island", "fsdp", None),
        P("island", "fsdp", None),
        P("island", None, "fsdp", None),
        P("island", None, "fsdp", None),
        P("island", None, "fsdp", None),
        P(None, "fsdp", None),
        P(None, "fsdp", None),
        P(),
    )
    return jax.shard_map(
        body,
        mesh=mesh,
        in_specs=placed,
        out_specs=(
            P("island", None, "fsdp", None),
            P("island", None, "fsdp", None),
            P("island", None, "fsdp", None),
            P(None, "fsdp", None),
            P(None, "fsdp", None),
        ),
        check_vma=False,
    )
```

```python
import functools

import jax
import jax.numpy as jnp
from jax import lax
from jax.experimental import pallas as pl
from jax.experimental.pallas import tpu as pltpu
from jax.sharding import PartitionSpec as P

HEAD = 128
LANES = 128
TOP = 32766.0
TINY = 1e-30
LIMIT = 6.0
F32 = jnp.float32
MESH = pl.DeviceIdType.MESH


def encode(value, codes, scales):
    @pl.loop(0, codes.shape[1] // LANES)
    def _(j):
        lanes = pl.ds(pl.multiple_of(j * LANES, LANES), LANES)
        v = value(lanes)
        top = jnp.maximum(jnp.max(jnp.abs(v), axis=0, keepdims=True), TINY)
        scales[:, lanes] = top * (1.0 / TOP)
        codes[:, lanes] = jnp.round(v * (TOP / top)).astype(jnp.int32).astype(jnp.int16)


def decode(codes, scales, lanes):
    return codes[:, lanes].astype(jnp.int32).astype(F32) * scales[:, lanes]


def grad_kernel(
    islands, rows, zrows, x_hbm, u_hbm, lw_hbm, first_hbm, second_hbm, anchor_hbm, moment_hbm, frag,
    grad, lwb, firstb, secondb, anchorb, momentb,
    xb, ub, part, own, core_in,
    zq, zs, zq_in, zs_in, wq, ws, wq_in, ws_in,
    xq, xs, xq_in, xs_in, yq, ys, yq_in, ys_in,
    mine, slots, half_sum, half_in, total,
    load_sem, state_sem, core_ss, core_rs, z_ss, z_rs, w_ss, w_rs, x_ss, x_rs, y_ss, y_rs, d_ss, d_rs,
):
    isl, place = lax.axis_index("island"), lax.axis_index("fsdp")
    z, x, c = place // 4, place // 2 % 2, place % 2
    y, h = isl // 2, isl % 2
    half = grad.shape[2]
    quarter = rows // 4
    reach = 4 * LIMIT

    def at(dz=0, dx=0, dc=0):
        return (isl, (z + dz) % 4 * 4 + (x + dx) % 2 * 2 + (c + dc) % 2)

    def island(dy=0, dh=0):
        return ((y + dy) % 4 * 2 + (h + dh) % 2, place)

    def order(k):
        dz = jnp.where(k < 2, 2, jnp.where(k >= 6, 0, jnp.where(k % 2 == 0, 1, 3)))
        dx = jnp.where(k < 2, 1 - k, jnp.where(k < 4, 1, jnp.where(k < 6, 0, 7 - k)))
        return (z + dz) % 4 * 2 + (x + dx) % 2

    def block(k, core):
        return pl.ds(pl.multiple_of((order(k) * 2 + core) * rows, rows), rows)

    def load_x(k, core):
        columns = block(k, (c + core) % 2)
        return pltpu.make_async_copy(x_hbm.at[0, :, columns], xb.at[:, columns], load_sem.at[k, core])

    def load_u(side):
        columns = pl.ds(side * half, half)
        return pltpu.make_async_copy(u_hbm.at[0, :, columns], ub.at[:, columns], load_sem.at[8, side])

    states = ((lw_hbm, lwb), (first_hbm, firstb), (second_hbm, secondb), (anchor_hbm, anchorb), (moment_hbm, momentb))
    load_states = [pltpu.make_async_copy(src, dst, state_sem.at[n]) for n, (src, dst) in enumerate(states)]
    load_u(0).start()
    load_x(0, 1).start()
    load_u(1).start()
    load_x(0, 0).start()

    barrier = pltpu.get_barrier_semaphore()
    peers = [at(dc=1), at(dx=1), at(dz=1), at(dz=3), island(1), island(2), island(3), island(dh=1)]
    for peer in peers:
        pl.semaphore_signal(barrier, inc=1, device_id=peer, device_id_type=MESH)

    def remote(src, dst, ss, rs, peer):
        return pltpu.make_async_remote_copy(
            src_ref=src, dst_ref=dst, send_sem=ss, recv_sem=rs, device_id=peer, device_id_type=MESH
        )

    def term(k, core, side=None):
        columns = pl.ds(0, 2 * half) if side is None else pl.ds(side * half, half)
        return lax.dot_general(
            xb[:, block(k, core)], ub[:, columns], (((0,), (0,)), ((), ())), preferred_element_type=F32
        )

    def store(terms, k, value):
        for side in (0, 1):
            terms[k, side] = value[:, side * half : (side + 1) * half]

    def core_copy(k, side):
        return remote(part.at[k, side], core_in.at[k, side], core_ss.at[k, side], core_rs.at[k, side], at(dc=1))

    def z_copy(d, s):
        peer = at(dz=1 if d == 0 else 3)
        return (
            remote(zq.at[d, s], zq_in.at[d, s], z_ss.at[d, s, 0], z_rs.at[d, s, 0], peer),
            remote(zs.at[d, s], zs_in.at[d, s], z_ss.at[d, s, 1], z_rs.at[d, s, 1], peer),
        )

    def w_copy(d, s):
        peer = at(dz=1 if d == 0 else 3)
        return (
            remote(wq.at[d, s], wq_in.at[d, s], w_ss.at[d, s, 0], w_rs.at[d, s, 0], peer),
            remote(ws.at[d, s], ws_in.at[d, s], w_ss.at[d, s, 1], w_rs.at[d, s, 1], peer),
        )

    def x_copy(s, side):
        peer = at(dx=1)
        return (
            remote(xq.at[s, side], xq_in.at[s, side], x_ss.at[s, side, 0], x_rs.at[s, side, 0], peer),
            remote(xs.at[s, side], xs_in.at[s, side], x_ss.at[s, side, 1], x_rs.at[s, side, 1], peer),
        )

    def y_copy(side):
        peer = at(dx=1)
        return (
            remote(yq.at[side], yq_in.at[side], y_ss.at[side, 0], y_rs.at[side, 0], peer),
            remote(ys.at[side], ys_in.at[side], y_ss.at[side, 1], y_rs.at[side, 1], peer),
        )

    def start(pair):
        for copy in pair:
            copy.start()

    def arrive(pair):
        for copy in pair:
            copy.wait_recv()

    def chip_term(k, r, n, side):
        return lambda lanes: own[k, side, pl.ds(r, n), lanes] + core_in[k, side, pl.ds(r, n), lanes]

    wrows = rows - zrows

    def z_term(k, side):
        return chip_term(k, 0, zrows, side)

    def w_term(k, slot, side):
        base = chip_term(k, zrows, wrows, side)

        return lambda lanes: base(lanes) + decode(xq_in.at[slot, side], xs_in.at[slot, side], lanes)

    def send_z(d, s, value):
        encode(value, zq.at[d, s], zs.at[d, s])
        start(z_copy(d, s))

    def send_w(d, s, value):
        encode(value, wq.at[d, s], ws.at[d, s])
        start(w_copy(d, s))

    def send_x(s, k, side):
        encode(chip_term(k, zrows, wrows, side), xq.at[s, side], xs.at[s, side])
        start(x_copy(s, side))

    def z_plus(d, k, got):
        arrive(z_copy(d, got))
        return lambda lanes: z_term(k, d)(lanes) + decode(zq_in.at[d, got], zs_in.at[d, got], lanes)

    load_x(0, 1).wait()
    for side in (0, 1):
        load_u(side).wait()
        part[0, side] = term(0, 1 - c, side)
        if side == 0:
            pl.semaphore_wait(barrier, len(peers))
        core_copy(0, side).start()

    for k in (1, 2):
        load_x(k, 1).start()
        load_x(k, 0).start()
    load_states[0].start()
    load_x(0, 0).wait()
    store(own, 0, term(0, c))
    for side in (0, 1):
        core_copy(0, side).wait_recv()
        send_z(side, 0, z_term(0, side))
        send_x(0, 0, side)

    @pl.loop(3, 8)
    def _(k):
        load_x(k, 1).start()
        load_x(k, 0).start()

    load_x(1, 1).wait()
    store(part, 1, term(1, 1 - c))
    for side in (0, 1):
        core_copy(1, side).start()

    load_states[0].wait()
    index = frag[0]
    heads = half // HEAD
    groups = [(p, pl.ds(j * HEAD, HEAD)) for p in range(lwb.shape[1]) for j in range(heads)]

    def fragment(array, few):
        chosen = array[0, few, groups[0][1]]
        for g, (p, lanes) in enumerate(groups[1:], 1):
            chosen = jnp.where(index == g, array[p, few, lanes], chosen)
        return chosen

    def by_rows(body):
        @pl.loop(0, rows // 32)
        def _(j):
            body(pl.ds(pl.multiple_of(j * 32, 32), 32))

    @by_rows
    def _(few):
        mine[few, :] = fragment(lwb.at[0], few)

    def y_rows(dy):
        return pl.ds(pl.multiple_of((y + dy) % 4 * quarter, quarter), quarter)

    def scatter_copy(dy):
        return remote(mine.at[y_rows(dy)], slots.at[dy - 1], d_ss.at[dy - 1], d_rs.at[dy - 1], island(dy))

    def cross_copy():
        return remote(half_sum, half_in, d_ss.at[3], d_rs.at[3], island(dh=1))

    def gather_copy(dy):
        return remote(total.at[y_rows(0)], total.at[y_rows(0)], d_ss.at[3 + dy], d_rs.at[3 + dy], island(dy))

    def gather_arrive(dy):
        rows_in = total.at[y_rows(-dy)]
        return remote(rows_in, rows_in, d_ss.at[3 + dy], d_rs.at[3 + dy], island(dy))

    for dy in (1, 2, 3):
        scatter_copy(dy).start()
    for copy in load_states[1:]:
        copy.start()

    def z_sum(k, leaf, chain, side):
        def value(lanes):
            return (
                z_term(k, side)(lanes)
                + decode(zq_in.at[side, chain], zs_in.at[side, chain], lanes)
                + decode(zq_in.at[1 - side, leaf], zs_in.at[1 - side, leaf], lanes)
            )

        return value

    def collect(side, r, n, value):
        @pl.loop(0, half // LANES)
        def _(j):
            lanes = pl.ds(pl.multiple_of(j * LANES, LANES), LANES)
            grad[side, pl.ds(r, n), lanes] = value(lanes)

    def add(side, r, n, value):
        @pl.loop(0, half // LANES)
        def _(j):
            lanes = pl.ds(pl.multiple_of(j * LANES, LANES), LANES)
            grad[side, pl.ds(r, n), lanes] += value(lanes)

    @pl.loop(1, 8)
    def _(k):
        @pl.when(k < 7)
        def _():
            load_x(k + 1, 1).wait()
            store(part, k + 1, term(k + 1, 1 - c))
            for side in (0, 1):
                core_copy(k + 1, side).start()

        load_x(k, 0).wait()
        store(own, k, term(k, c))
        for side in (0, 1):
            core_copy(k, side).wait_recv()

        @pl.when(k == 1)
        def _():
            send_z(0, 1, z_term(1, 0))
            send_z(1, 1, z_term(1, 1))

        @pl.when(k == 2)
        def _():
            send_z(0, 2, z_term(2, 1))
            send_x(1, 2, 0)
            send_x(1, 2, 1)

        @pl.when(k == 3)
        def _():
            send_z(1, 2, z_term(3, 0))
            for dy in (1, 2, 3):
                scatter_copy(dy).wait_recv()
            column = mine[y_rows(0), :] + slots[0] + slots[1] + slots[2]
            half_sum[...] = jnp.round(column * (TOP / reach)).astype(jnp.int32).astype(jnp.int16)
            cross_copy().start()
            send_x(2, 3, 0)
            send_x(2, 3, 1)
            send_z(0, 3, z_plus(0, 2, 0))
            send_z(1, 3, z_plus(1, 3, 0))

        @pl.when(k == 4)
        def _():
            send_z(0, 4, z_term(4, 1))

        @pl.when(k == 5)
        def _():
            send_z(1, 4, z_term(5, 0))
            for d in (0, 1):
                arrive(x_copy(0, d))
                send_w(d, 0, w_term(1, 0, d))
            send_z(0, 5, z_plus(0, 4, 1))
            send_z(1, 5, z_plus(1, 5, 1))

        @pl.when(k == 6)
        def _():
            send_x(3, 6, 0)
            send_x(3, 6, 1)
            arrive(x_copy(1, 0))
            arrive(x_copy(1, 1))
            send_w(0, 1, w_term(4, 1, 1))

    for d in (0, 1):
        arrive(z_copy(d, 2))
        arrive(z_copy(d, 3))
    for side in (0, 1):
        encode(z_sum(6, 2, 3, side), yq.at[side], ys.at[side])
        start(y_copy(side))

    cross_copy().wait_recv()
    total[y_rows(0), :] = (half_sum[...].astype(jnp.int32) + half_in[...].astype(jnp.int32)).astype(F32) * (reach / TOP)
    for dy in (1, 2, 3):
        gather_copy(dy).start()

    arrive(x_copy(2, 0))
    arrive(x_copy(2, 1))
    send_w(1, 1, w_term(5, 2, 0))
    for d, k, slot in ((0, 4, 1), (1, 5, 2)):
        arrive(w_copy(d, 0))
        base = w_term(k, slot, d)
        send_w(d, 2, lambda lanes, d=d, base=base: base(lanes) + decode(wq_in.at[d, 0], ws_in.at[d, 0], lanes))

    for dy in (1, 2, 3):
        gather_arrive(dy).wait_recv()
    for copy in load_states[1:]:
        copy.wait()

    @by_rows
    def _(few):
        anchor_f = fragment(anchorb, few)
        drift = anchor_f - total[few, :] * (1.0 / islands)
        moment_f = 0.9 * fragment(momentb, few) + drift
        merged = anchor_f - 0.7 * (0.9 * moment_f + drift)
        for g, (p, lanes) in enumerate(groups):
            here = index == g
            anchorb[p, few, lanes] = jnp.where(here, merged, anchorb[p, few, lanes])
            momentb[p, few, lanes] = jnp.where(here, moment_f, momentb[p, few, lanes])
            lwb[0, p, few, lanes] = jnp.where(here, merged, lwb[0, p, few, lanes])

    for d in (0, 1):
        arrive(z_copy(d, 4))
        arrive(z_copy(d, 5))
    for side in (0, 1):
        collect(side, 0, zrows, z_sum(7, 4, 5, side))
    arrive(x_copy(3, 0))
    arrive(x_copy(3, 1))
    for d in (0, 1):
        arrive(w_copy(d, 1))
    for side in (0, 1):
        base = w_term(7, 3, side)
        collect(
            side, zrows, wrows,
            lambda lanes, side=side, base=base: base(lanes)
            + decode(wq_in.at[1 - side, 1], ws_in.at[1 - side, 1], lanes),
        )
    def finish(pairs):
        for pair in pairs:
            for copy in pair:
                copy.wait_send()

    finish([[scatter_copy(dy), gather_copy(dy)] for dy in (1, 2, 3)] + [[cross_copy()]])

    @pl.loop(0, 8)
    def _(k):
        finish([[core_copy(k, side) for side in (0, 1)]])

    finish([z_copy(d, s) for d in (0, 1) for s in range(6)] + [w_copy(d, s) for d in (0, 1) for s in (0, 1)])
    finish([x_copy(s, side) for s in range(4) for side in (0, 1)])

    for d in (0, 1):
        arrive(w_copy(d, 2))
    for side in (0, 1):
        add(side, zrows, wrows, lambda lanes, side=side: decode(wq_in.at[side, 2], ws_in.at[side, 2], lanes))
    for side in (0, 1):
        arrive(y_copy(side))
        add(side, 0, zrows, lambda lanes, side=side: decode(yq_in.at[side], ys_in.at[side], lanes))

    finish([w_copy(d, 2) for d in (0, 1)] + [y_copy(side) for side in (0, 1)])


def update_kernel(
    step, grad, lw, first, second, anchor, moment,
    lw_out, first_out, second_out, anchor_out, moment_out, lw_new, first_new, second_new, sems, shared_sems,
):
    shared = [
        pltpu.make_async_copy(src, dst, shared_sems.at[n])
        for n, (src, dst) in enumerate(((anchor, anchor_out), (moment, moment_out)))
    ]
    for copy in shared:
        copy.start()
    frags, rows, half = grad.shape
    groups = [(p, pl.ds(j * LANES, LANES)) for p in range(frags) for j in range(half // LANES)]

    def copies(i):
        some = pl.ds(pl.multiple_of(i * step, step), step)
        pairs = [(lw_new, lw_out.at[0]), (first_new, first_out.at[0]), (second_new, second_out.at[0])]
        return [
            pltpu.make_async_copy(src.at[:, some], dst.at[:, some], sems.at[i, n]) for n, (src, dst) in enumerate(pairs)
        ]

    @pl.loop(0, rows // step)
    def _(i):
        some = pl.ds(pl.multiple_of(i * step, step), step)
        for p, lanes in groups:
            gr = grad[p, some, lanes]
            begin = lw[0, p, some, lanes]
            m = 0.9 * first[0, p, some, lanes] + 0.1 * gr
            v = 0.95 * second[0, p, some, lanes] + 0.05 * gr * gr
            first_new[p, some, lanes] = m
            second_new[p, some, lanes] = v
            lw_new[p, some, lanes] = begin - 0.02 * (m / (jnp.sqrt(v) + 1e-08) + 0.1 * begin)
        for copy in copies(i):
            copy.start()

    @pl.loop(0, rows // step)
    def _(i):
        for copy in copies(i):
            copy.wait()

    for copy in shared:
        copy.wait()


def body(features, upstream, local_weights, first_moment, second_moment, anchor, outer_momentum, fragment):
    _, tokens, width = features.shape
    _, frags, rows, half = local_weights.shape
    cols = frags * half
    zrows = rows * 9 // 16
    wrows = rows - zrows
    i16 = jnp.int16

    def vm(shape, dtype):
        return pltpu.VMEM(shape, dtype)

    def both(*shape):
        return [vm(shape, i16), vm(shape[:-2] + (1, shape[-1]), F32)] * 2

    def sems(*shape):
        return pltpu.SemaphoreType.DMA(shape)

    states = (local_weights, first_moment, second_moment, anchor, outer_momentum)
    any_space = pl.BlockSpec(memory_space=pl.ANY)
    near = pl.pallas_call(
        functools.partial(grad_kernel, lax.axis_size("island"), rows, zrows),
        out_shape=(vm((frags, rows, half), F32), *[vm(a.shape, F32) for a in states]),
        in_specs=[any_space] * 7 + [pl.BlockSpec(memory_space=pltpu.SMEM)],
        out_specs=[pl.BlockSpec(memory_space=pltpu.VMEM)] * 6,
        scratch_shapes=[
            vm((tokens, width), jnp.bfloat16),
            vm((tokens, cols), jnp.bfloat16),
            vm((8, frags, rows, half), F32),
            vm((8, frags, rows, half), F32),
            vm((8, frags, rows, half), F32),
            *both(2, 6, zrows, half),
            *both(2, 3, wrows, half),
            *both(4, 2, wrows, half),
            *both(2, zrows, half),
            vm((rows, HEAD), F32),
            vm((3, rows // 4, HEAD), F32),
            vm((rows // 4, HEAD), i16),
            vm((rows // 4, HEAD), i16),
            vm((rows, HEAD), F32),
            sems(9, 2),
            sems(5),
            sems(8, 2),
            sems(8, 2),
            sems(2, 6, 2),
            sems(2, 6, 2),
            sems(2, 3, 2),
            sems(2, 3, 2),
            sems(4, 2, 2),
            sems(4, 2, 2),
            sems(2, 2),
            sems(2, 2),
            sems(7),
            sems(7),
        ],
        compiler_params=pltpu.CompilerParams(
            collective_id=0, has_side_effects=True, vmem_limit_bytes=48 * 2**20
        ),
    )(features, upstream, *states, fragment)

    step = rows // 8
    weights_shape = jax.ShapeDtypeStruct(local_weights.shape, F32)
    anchor_shape = jax.ShapeDtypeStruct(anchor.shape, F32)
    return pl.pallas_call(
        functools.partial(update_kernel, step),
        out_shape=(weights_shape, weights_shape, weights_shape, anchor_shape, anchor_shape),
        in_specs=[pl.BlockSpec(memory_space=pltpu.VMEM)] * 6,
        out_specs=[any_space] * 5,
        scratch_shapes=[vm((frags, rows, half), F32)] * 3 + [sems(8, 3), sems(2)],
        compiler_params=pltpu.CompilerParams(vmem_limit_bytes=16 * 2**20),
    )(*[pltpu.with_memory_space_constraint(a, pltpu.VMEM) for a in near])


def solution(mesh):
    placed = (
        P("island", "fsdp", None),
        P("island", "fsdp", None),
        P("island", None, "fsdp", None),
        P("island", None, "fsdp", None),
        P("island", None, "fsdp", None),
        P(None, "fsdp", None),
        P(None, "fsdp", None),
        P(),
    )
    return jax.shard_map(
        body,
        mesh=mesh,
        in_specs=placed,
        out_specs=(
            P("island", None, "fsdp", None),
            P("island", None, "fsdp", None),
            P("island", None, "fsdp", None),
            P(None, "fsdp", None),
            P(None, "fsdp", None),
        ),
        check_vma=False,
    )
```
